32 devices in a mesh: mat: 4 (over y, x), gr: 4 (over z), gc: 2 (over core).
Axes of the slice: x: 2, y: 2, z: 4, core: 2. Of those that a mesh axis runs over, the one named last changes fastest.
Arguments:
- iterate: bfloat16 [2, 4, 512, 7168], P(None, 'gr', ('mat', 'gc')), may hold values from -3 to 3
Outputs:
- next_iterate: bfloat16 [2, 2048, 7168], P(None, 'gr', ('mat', 'gc'))
The draws below stay inside these ranges and needn't reach their ends.
All inputs are finite; a program needn't handle non-finite values.
Results may differ from the reference program's by a relative error of at most 0.0055.
Values may be sent and summed in bfloat16 or wider, within the bound.
No kernel may reach another device: no remote copies, remote signals or barrier semaphores. Data moves between devices by JAX's collectives and lax.ppermute only.
A program may use at most 64 MiB of HBM per device.

```python
import jax
import jax.numpy as jnp
from jax import lax

M = 2048
N = 7168
MATS = 2
RB = 512
N_GR = 4


def draw_iterate(key, part):
    base_key = jax.random.fold_in(key, 21)
    shape = (MATS, N_GR, RB, N)
    values = 0.7 * jnp.clip(jax.random.normal(base_key, shape, jnp.float32), -4.0, 4.0)
    return values.astype(jnp.bfloat16)


def setup_inputs(seed: int = 0) -> dict:
    key_of = jax.random.split(jax.random.key(seed), 2)
    iterate = draw_iterate(jax.random.fold_in(key_of[1], 71), 0)
    return {"iterate": iterate}


linear_coef = 3.4445
cubic_coef = -4.7750
quintic_coef = 2.0315


def one_matrix(blocks):
    grad = blocks.reshape(M, N)
    gram_sum = lax.dot_general(grad, grad, (((1,), (1,)), ((), ())), preferred_element_type=jnp.float32) * (1.0 / N)
    gram = gram_sum.astype(jnp.bfloat16)
    square = jnp.dot(gram, gram, preferred_element_type=jnp.float32)
    poly = (cubic_coef * gram.astype(jnp.float32) + quintic_coef * square).astype(jnp.bfloat16)
    mixed = jnp.dot(poly, grad, preferred_element_type=jnp.float32)
    result = linear_coef * grad.astype(jnp.float32) + mixed
    return result.astype(jnp.bfloat16)


def reference(iterate):
    return lax.map(one_matrix, iterate)
```

```python
import functools

import jax
import jax.numpy as jnp
from jax import lax
from jax.experimental import pallas as pl
from jax.experimental.pallas import tpu as pltpu
from jax.sharding import PartitionSpec as P

linear_coef = 3.4445
cubic_coef = -4.775
quintic_coef = 2.0315

AXES = ("mat", "gr", "gc")


def plain_body(iterate):
    regrouped = lax.all_to_all(iterate, ("mat", "gc"), split_axis=3, concat_axis=2, tiled=True)
    row_block = regrouped[:, 0]
    panel_rows = lax.all_gather(row_block, "gr", axis=1, tiled=True)
    total_rows = panel_rows.shape[1]
    groups = lax.axis_size(("mat", "gc"))
    gram_width = total_rows // groups
    inv_cols = 1.0 / iterate.shape[-1]
    partial_value = jnp.einsum(
        "irc,ijc->irj", row_block, panel_rows, preferred_element_type=jnp.float32
    )
    gram_rows = (lax.psum(partial_value, ("mat", "gc")) * inv_cols).astype(jnp.bfloat16)
    own_block = lax.dynamic_slice_in_dim(
        gram_rows, lax.axis_index(("mat", "gc")) * gram_width, gram_width, 2
    )
    square = jnp.einsum(
        "irk,ikj->irj",
        gram_rows,
        lax.all_gather(own_block, "gr", axis=1, tiled=True),
        preferred_element_type=jnp.float32,
    )
    poly_block = (cubic_coef * own_block.astype(jnp.float32) + quintic_coef * square).astype(
        jnp.bfloat16
    )
    mixed_sum = jnp.einsum(
        "irk,ikc->irc",
        lax.all_gather(poly_block, ("mat", "gc"), axis=2, tiled=True),
        panel_rows,
        preferred_element_type=jnp.float32,
    )
    result = linear_coef * row_block.astype(jnp.float32) + mixed_sum
    return result.astype(jnp.bfloat16)


CHIPS = 8
BLOCK = 128
STRIP = 9 * BLOCK
PARAMS = dict(vmem_limit_bytes=48 * 1024 * 1024)


def send(value, move):
    perm = []
    for m in range(4):
        for r in range(4):
            for c in range(2):
                to = move(m, r, c)
                perm.append((m * 8 + r * 2 + c, to[0] * 8 + to[1] * 2 + to[2]))
    return lax.ppermute(value, AXES, perm)


def across(d):
    return lambda m, r, c: (m ^ (d >> 1), r ^ (d & 1), c)


def other_core(m, r, c):
    return m, r, 1 - c


def cut_kernel(x_ref, o_ref, sems):
    copies = []
    width = o_ref.shape[-1]
    for q in range(2):
        for k in range(CHIPS):
            copies.append(
                pltpu.make_async_copy(
                    x_ref.at[q, :, pl.ds(k * width, width)],
                    o_ref.at[q, k % 2, k // 2],
                    sems.at[q * CHIPS + k],
                )
            )
    for copy in copies:
        copy.start()
    for copy in copies:
        copy.wait()


def cut(x):
    _, rows, cols = x.shape
    return pl.pallas_call(
        cut_kernel,
        out_shape=jax.ShapeDtypeStruct((2, 2, 4, rows, cols // CHIPS), x.dtype),
        in_specs=[pl.BlockSpec(memory_space=pl.ANY)],
        out_specs=pl.BlockSpec(memory_space=pl.ANY),
        scratch_shapes=[pltpu.SemaphoreType.DMA((16,))],
        compiler_params=pltpu.CompilerParams(**PARAMS),
        name="cut_columns",
    )(x)


def gram_kernel(p_ref, own_ref, other_ref, *rest):
    outs, strips = rest[:CHIPS], rest[CHIPS]
    dims = (((1,), (1,)), ((), ()))
    for t in range(4):
        lo = 256 * t
        rows = own_ref[lo : lo + 256, :]
        mine = lax.dot_general(rows, own_ref[lo:1024, :], dims, preferred_element_type=jnp.float32)
        theirs = lax.dot_general(
            rows, other_ref[0 : lo + 256, :], dims, preferred_element_type=jnp.float32
        )
        both = jnp.concatenate([mine, theirs], axis=1).astype(jnp.bfloat16)
        strips[2 * t] = both[:128, :STRIP]
        strips[2 * t + 1] = both[128:, 128 : 128 + STRIP]
    p = p_ref[0]
    for d in range(CHIPS):
        outs[d][...] = strips[p ^ d]


def gram_strips(p, own, other):
    return pl.pallas_call(
        gram_kernel,
        out_shape=[jax.ShapeDtypeStruct((BLOCK, STRIP), jnp.bfloat16)] * CHIPS,
        in_specs=[pl.BlockSpec(memory_space=pltpu.SMEM)]
        + [pl.BlockSpec(memory_space=pltpu.VMEM)] * 2,
        out_specs=[pl.BlockSpec(memory_space=pltpu.VMEM)] * CHIPS,
        scratch_shapes=[pltpu.VMEM((CHIPS, BLOCK, STRIP), jnp.bfloat16)],
        compiler_params=pltpu.CompilerParams(**PARAMS),
        name="gram_strips",
    )(p, own, other)


def add_kernel(scale, *refs):
    total = refs[0][...].astype(jnp.float32)
    for ref in refs[1:-1]:
        total += ref[...].astype(jnp.float32)
    refs[-1][...] = (total * scale).astype(jnp.bfloat16)


def add_strips(parts, scale):
    return pl.pallas_call(
        functools.partial(add_kernel, scale),
        out_shape=jax.ShapeDtypeStruct((BLOCK, STRIP), jnp.bfloat16),
        in_specs=[pl.BlockSpec(memory_space=pltpu.VMEM)] * CHIPS,
        out_specs=pl.BlockSpec(memory_space=pltpu.VMEM),
        compiler_params=pltpu.CompilerParams(**PARAMS),
        name="add_strips",
    )(*parts)


def stack_kernel(p_ref, *refs):
    parts, out, sems = refs[:CHIPS], refs[CHIPS], refs[CHIPS + 1]
    p = p_ref[0]
    copies = [
        pltpu.make_async_copy(parts[d], out.at[p ^ d], sems.at[d]) for d in range(CHIPS)
    ]
    for copy in copies:
        copy.start()
    for copy in copies:
        copy.wait()


def stack_strips(p, parts):
    return pl.pallas_call(
        stack_kernel,
        out_shape=jax.ShapeDtypeStruct((CHIPS, BLOCK, STRIP), jnp.bfloat16),
        in_specs=[pl.BlockSpec(memory_space=pltpu.SMEM)]
        + [pl.BlockSpec(memory_space=pl.ANY)] * CHIPS,
        out_specs=pl.BlockSpec(memory_space=pl.ANY),
        scratch_shapes=[pltpu.SemaphoreType.DMA((CHIPS,))],
        compiler_params=pltpu.CompilerParams(**PARAMS),
        name="stack_strips",
    )(p, *parts)


def poly_kernel(
    s_ref, a_ref, b_ref, own_ref, other_ref, far_ref, near_ref, gram, poly
):
    for i in range(CHIPS):
        lo = BLOCK * i
        gram[lo : lo + BLOCK, lo : lo + STRIP] = a_ref[i]
        gram[lo + BLOCK : lo + 1024, lo : lo + BLOCK] = a_ref[i][:, BLOCK:1024].T
        rows = slice(1024 + lo, 1024 + lo + BLOCK)
        left = 1024 - lo
        gram[rows, 1024 + lo : 2048] = b_ref[i][:, :left]
        gram[rows, 0 : BLOCK + lo] = b_ref[i][:, left:]
        if left > BLOCK:
            gram[1024 + lo + BLOCK : 2048, rows] = b_ref[i][:, BLOCK:left].T
        if i:
            gram[0:lo, rows] = b_ref[i][:, left:1024].T
    core = s_ref[1]
    for out, place in ((far_ref, s_ref[2]), (near_ref, s_ref[3])):
        for half, (panel, sub) in enumerate(((own_ref, core), (other_ref, 1 - core))):
            start = pl.multiple_of(place * 256, 256)
            rows = gram[pl.ds(1024 * half + start, 256), :]
            for n in range(0, 2048, 512):
                square = jnp.dot(rows, gram[:, n : n + 512], preferred_element_type=jnp.float32)
                poly[:, n : n + 512] = (
                    cubic_coef * rows[:, n : n + 512].astype(jnp.float32) + quintic_coef * square
                ).astype(jnp.bfloat16)
            mixed = jnp.dot(poly[:, :1024], own_ref[...], preferred_element_type=jnp.float32)
            mixed += jnp.dot(poly[:, 1024:], other_ref[...], preferred_element_type=jnp.float32)
            result = linear_coef * panel[pl.ds(start, 256), :].astype(jnp.float32) + mixed
            result = result.astype(jnp.bfloat16).reshape(8, 1, 32, result.shape[-1])
            out[:, pl.ds(sub, 1)] = result


def poly_rows(scalars, strips, strips_other, own, other):
    width = own.shape[-1]
    piece = jax.ShapeDtypeStruct((8, 2, 32, width), jnp.bfloat16)
    return pl.pallas_call(
        poly_kernel,
        out_shape=[piece, piece],
        in_specs=[pl.BlockSpec(memory_space=pltpu.SMEM)]
        + [pl.BlockSpec(memory_space=pltpu.VMEM)] * 4,
        out_specs=[pl.BlockSpec(memory_space=pltpu.VMEM)] * 2,
        scratch_shapes=[
            pltpu.VMEM((2048, 2048), jnp.bfloat16),
            pltpu.VMEM((256, 2048), jnp.bfloat16),
        ],
        compiler_params=pltpu.CompilerParams(**PARAMS),
        name="poly_rows",
    )(scalars, strips, strips_other, own, other)


def fast_body(iterate):
    x = iterate[:, 0]
    mats, rows, cols = x.shape
    m, r, c = (lax.axis_index(axis) for axis in AXES)
    q, b = r // 2, r % 2
    scalars = jnp.stack([2 * m + b, c, 2 * (1 - q) + c, 2 * q + c]).astype(jnp.int32)
    pieces = cut(x).reshape(32, rows // 2, cols // CHIPS)
    own = lax.all_to_all(pieces, ("gr", "mat", "gc"), 0, 0, tiled=True)
    own = own.reshape(1024, cols // CHIPS)
    other = send(own, other_core)
    parts = gram_strips(scalars, own, other)
    parts = [parts[0]] + [send(parts[d], across(d)) for d in range(1, CHIPS)]
    strip = add_strips(parts, 1.0 / cols)
    strips = stack_strips(scalars, [strip] + [send(strip, across(d)) for d in range(1, CHIPS)])
    strips_other = send(strips, other_core)
    far, near = poly_rows(scalars, strips, strips_other, own, other)
    far = send(far, lambda m, r, c: (m, (1 - r // 2) * 2 + c, r % 2))
    near = send(near, lambda m, r, c: (m, (r // 2) * 2 + c, r % 2))
    far, near = (v.reshape(1, 512, cols // CHIPS) for v in (far, near))
    first, second = lax.cond(q == 0, lambda: (near, far), lambda: (far, near))
    return jnp.concatenate([first, second], axis=0)


def solution(mesh):
    fast = tuple(mesh.shape[axis] for axis in AXES) == (4, 4, 2)
    return jax.shard_map(
        fast_body if fast else plain_body,
        mesh=mesh,
        in_specs=(P(None, "gr", ("mat", "gc"), None),),
        out_specs=P(None, "gr", ("mat", "gc")),
        check_vma=False,
    )
```

```python
import functools

import jax
import jax.numpy as jnp
from jax import lax
from jax.experimental import pallas as pl
from jax.experimental.pallas import tpu as pltpu
from jax.sharding import PartitionSpec as P

linear_coef = 3.4445
cubic_coef = -4.775
quintic_coef = 2.0315

AXES = ("mat", "gr", "gc")


def plain_body(iterate):
    regrouped = lax.all_to_all(iterate, ("mat", "gc"), split_axis=3, concat_axis=2, tiled=True)
    row_block = regrouped[:, 0]
    panel_rows = lax.all_gather(row_block, "gr", axis=1, tiled=True)
    total_rows = panel_rows.shape[1]
    groups = lax.axis_size(("mat", "gc"))
    gram_width = total_rows // groups
    inv_cols = 1.0 / iterate.shape[-1]
    partial_value = jnp.einsum(
        "irc,ijc->irj", row_block, panel_rows, preferred_element_type=jnp.float32
    )
    gram_rows = (lax.psum(partial_value, ("mat", "gc")) * inv_cols).astype(jnp.bfloat16)
    own_block = lax.dynamic_slice_in_dim(
        gram_rows, lax.axis_index(("mat", "gc")) * gram_width, gram_width, 2
    )
    square = jnp.einsum(
        "irk,ikj->irj",
        gram_rows,
        lax.all_gather(own_block, "gr", axis=1, tiled=True),
        preferred_element_type=jnp.float32,
    )
    poly_block = (cubic_coef * own_block.astype(jnp.float32) + quintic_coef * square).astype(
        jnp.bfloat16
    )
    mixed_sum = jnp.einsum(
        "irk,ikc->irc",
        lax.all_gather(poly_block, ("mat", "gc"), axis=2, tiled=True),
        panel_rows,
        preferred_element_type=jnp.float32,
    )
    result = linear_coef * row_block.astype(jnp.float32) + mixed_sum
    return result.astype(jnp.bfloat16)


CHIPS = 8
BLOCK = 128
STRIP = 9 * BLOCK
THIRD = STRIP // 3
ORDERS = ((2, 4, 1), (4, 1, 2), (1, 2, 4))
PARAMS = dict(vmem_limit_bytes=28 * 1024 * 1024)


def cost(flops, bytes_accessed):
    return pl.CostEstimate(flops=flops, bytes_accessed=bytes_accessed, transcendentals=0)


def offset(third, place):
    axes = ORDERS[third]
    return sum(axes[k] for k in range(3) if place >> (2 - k) & 1)


def send(value, move):
    perm = []
    for m in range(4):
        for r in range(4):
            for c in range(2):
                to = move(m, r, c)
                perm.append((m * 8 + r * 2 + c, to[0] * 8 + to[1] * 2 + to[2]))
    return lax.ppermute(value, AXES, perm)


def across(d):
    return lambda m, r, c: (m ^ (d >> 1), r ^ (d & 1), c)


def other_core(m, r, c):
    return m, r, 1 - c


def cut_kernel(x_ref, o_ref, sems):
    copies = []
    width = o_ref.shape[-1]
    for q in range(2):
        for k in range(CHIPS):
            copies.append(
                pltpu.make_async_copy(
                    x_ref.at[q, :, pl.ds(k * width, width)],
                    o_ref.at[q, k % 2, k // 2],
                    sems.at[q * CHIPS + k],
                )
            )
    for copy in copies:
        copy.start()
    for copy in copies:
        copy.wait()


def cut(x):
    _, rows, cols = x.shape
    return pl.pallas_call(
        cut_kernel,
        out_shape=jax.ShapeDtypeStruct((2, 2, 4, rows, cols // CHIPS), x.dtype),
        in_specs=[pl.BlockSpec(memory_space=pl.ANY)],
        out_specs=pl.BlockSpec(memory_space=pl.ANY),
        scratch_shapes=[pltpu.SemaphoreType.DMA((16,))],
        compiler_params=pltpu.CompilerParams(**PARAMS),
        name="cut_columns",
    )(x)


def gram_kernel(p_ref, own_ref, other_ref, *rest):
    keep, away, strips = rest[:3], rest[3:6], rest[6]
    dims = (((1,), (1,)), ((), ()))
    for t in range(4):
        lo = 256 * t
        rows = own_ref[lo : lo + 256, :]
        mine = lax.dot_general(rows, own_ref[lo:1024, :], dims, preferred_element_type=jnp.float32)
        theirs = lax.dot_general(
            rows, other_ref[0 : lo + 256, :], dims, preferred_element_type=jnp.float32
        )
        both = jnp.concatenate([mine, theirs], axis=1)
        strips[2 * t] = both[:128, :STRIP]
        strips[2 * t + 1] = both[128:, 128 : 128 + STRIP]
    p = p_ref[0]
    for i in range(3):
        cols = slice(THIRD * i, THIRD * (i + 1))
        for place in range(4):
            keep[i][place] = strips[p ^ offset(i, place), :, cols]
            away[i][place] = strips[p ^ offset(i, place + 4), :, cols].astype(jnp.bfloat16)


def gram_strips(p, own, other):
    shape = (4, BLOCK, THIRD)
    return pl.pallas_call(
        gram_kernel,
        out_shape=[jax.ShapeDtypeStruct(shape, jnp.float32)] * 3
        + [jax.ShapeDtypeStruct(shape, jnp.bfloat16)] * 3,
        in_specs=[pl.BlockSpec(memory_space=pltpu.SMEM)]
        + [pl.BlockSpec(memory_space=pltpu.VMEM)] * 2,
        out_specs=[pl.BlockSpec(memory_space=pltpu.VMEM)] * 6,
        scratch_shapes=[pltpu.VMEM((CHIPS, BLOCK, STRIP), jnp.float32)],
        compiler_params=pltpu.CompilerParams(**PARAMS),
        cost_estimate=cost(2 * 1024 * 1280 * own.shape[-1], 10**7),
        name="gram_strips",
    )(p, own, other)


def halves_kernel(*refs):
    held, came, keep, away = (refs[3 * k : 3 * k + 3] for k in range(4))
    for i in range(3):
        half = keep[i].shape[0]
        total = held[i][...] + came[i][...].astype(jnp.float32)
        keep[i][...] = total[:half]
        away[i][...] = total[half:].astype(jnp.bfloat16)


def pairs_kernel(*refs):
    held, came, keep, away = (refs[3 * k : 3 * k + 3] for k in range(4))
    for i in range(3):
        total = held[i][...] + came[i][...].astype(jnp.float32)
        keep[i][...] = total
        away[i][0] = total[1].astype(jnp.bfloat16)
        away[i][1] = total[0].astype(jnp.bfloat16)


def add_step(kernel, name, held, came, count):
    shape = (count, BLOCK, THIRD)
    made = pl.pallas_call(
        kernel,
        out_shape=[jax.ShapeDtypeStruct(shape, jnp.float32)] * 3
        + [jax.ShapeDtypeStruct(shape, jnp.bfloat16)] * 3,
        in_specs=[pl.BlockSpec(memory_space=pltpu.VMEM)] * 6,
        out_specs=[pl.BlockSpec(memory_space=pltpu.VMEM)] * 6,
        compiler_params=pltpu.CompilerParams(**PARAMS),
        name=name,
    )(*held, *came)
    return made[:3], made[3:]


def add_halves(held, came):
    return add_step(halves_kernel, "add_halves", held, came, 2)


def add_pairs(held, came):
    return add_step(pairs_kernel, "add_pairs", held, came, 2)


def last_kernel(scale, *refs):
    held, came, outs = refs[:3], refs[3:6], refs[6:]
    for i in range(3):
        total = held[i][...] + came[i][...].astype(jnp.float32)
        outs[i][...] = (total * scale).astype(jnp.bfloat16)


def add_last(held, came, scale):
    return pl.pallas_call(
        functools.partial(last_kernel, scale),
        out_shape=[jax.ShapeDtypeStruct(held[0].shape, jnp.bfloat16)] * 3,
        in_specs=[pl.BlockSpec(memory_space=pltpu.VMEM)] * 6,
        out_specs=[pl.BlockSpec(memory_space=pltpu.VMEM)] * 3,
        compiler_params=pltpu.CompilerParams(**PARAMS),
        name="add_last",
    )(*held, *came)


def sum_strips(keep, away, scale):
    came = [send(away[i], across(ORDERS[i][0])) for i in range(3)]
    keep, away = add_halves(keep, came)
    came = [send(away[i], across(ORDERS[i][1])) for i in range(3)]
    keep, away = add_pairs(keep, came)
    came = [send(away[i], across(ORDERS[i][2])) for i in range(3)]
    return add_last(keep, came, scale)


def gather_strips(parts):
    came = [send(parts[i], across(ORDERS[i][1])) for i in range(3)]
    parts = [jnp.concatenate([parts[i], came[i]], axis=0) for i in range(3)]
    late = [send(parts[i], across(ORDERS[i][0])) for i in range(3)]
    early_other = [send(part, other_core) for part in parts]
    late_other = [send(part, other_core) for part in late]
    return parts + late, early_other + late_other


def result_rows(gram, panels, poly, place, half):
    start = pl.multiple_of(place * 256, 256)
    rows = gram[pl.ds(1024 * half + start, 256), :]
    for n in range(0, 2048, 512):
        square = jnp.dot(rows, gram[:, n : n + 512], preferred_element_type=jnp.float32)
        poly[:, n : n + 512] = (
            cubic_coef * rows[:, n : n + 512].astype(jnp.float32) + quintic_coef * square
        ).astype(jnp.bfloat16)
    mixed = jnp.dot(poly[:, :1024], panels[0][...], preferred_element_type=jnp.float32)
    mixed += jnp.dot(poly[:, 1024:], panels[1][...], preferred_element_type=jnp.float32)
    return (linear_coef * panels[half][pl.ds(start, 256), :].astype(jnp.float32) + mixed).astype(
        jnp.bfloat16
    )


def first_kernel(s_ref, *refs):
    thirds, others, panels = refs[:6], refs[6:12], refs[12:14]
    gram, out, own, other, poly = refs[14:]
    p = s_ref[0]
    for i in range(3):
        cols = slice(THIRD * i, THIRD * (i + 1))
        for place in range(CHIPS):
            for strips, source in ((own, thirds), (other, others)):
                strips[p ^ offset(i, place), :, cols] = source[i + 3 * (place // 4)][place % 4]
    for i in range(CHIPS):
        lo = BLOCK * i
        gram[lo : lo + BLOCK, lo : lo + STRIP] = own[i]
        gram[lo + BLOCK : lo + 1024, lo : lo + BLOCK] = own[i][:, BLOCK:1024].T
        rows = slice(1024 + lo, 1024 + lo + BLOCK)
        left = 1024 - lo
        gram[rows, 1024 + lo : 2048] = other[i][:, :left]
        gram[rows, 0 : BLOCK + lo] = other[i][:, left:]
        if left > BLOCK:
            gram[1024 + lo + BLOCK : 2048, rows] = other[i][:, BLOCK:left].T
        if i:
            gram[0:lo, rows] = other[i][:, left:1024].T
    for half in range(2):
        out[256 * half : 256 * (half + 1)] = result_rows(gram, panels, poly, s_ref[1], half)


def first_rows(scalars, thirds, others, panels):
    cols = panels[0].shape[-1]
    return pl.pallas_call(
        first_kernel,
        out_shape=[
            jax.ShapeDtypeStruct((2048, 2048), jnp.bfloat16),
            jax.ShapeDtypeStruct((512, cols), jnp.bfloat16),
        ],
        in_specs=[pl.BlockSpec(memory_space=pltpu.SMEM)]
        + [pl.BlockSpec(memory_space=pltpu.VMEM)] * 14,
        out_specs=[pl.BlockSpec(memory_space=pltpu.VMEM)] * 2,
        scratch_shapes=[pltpu.VMEM((CHIPS, BLOCK, STRIP), jnp.bfloat16)] * 2
        + [pltpu.VMEM((256, 2048), jnp.bfloat16)],
        compiler_params=pltpu.CompilerParams(**PARAMS),
        cost_estimate=cost(2 * 512 * 2048 * (2048 + cols), 3 * 10**7),
        name="first_rows",
    )(scalars, *thirds, *others, *panels)


def near_kernel(s_ref, gram, own, other, out, poly):
    for half in range(2):
        out[256 * half : 256 * (half + 1)] = result_rows(
            gram, (own, other), poly, s_ref[2], half
        )


def near_rows(scalars, gram, panels):
    cols = panels[0].shape[-1]
    return pl.pallas_call(
        near_kernel,
        out_shape=jax.ShapeDtypeStruct((512, cols), jnp.bfloat16),
        in_specs=[pl.BlockSpec(memory_space=pltpu.SMEM)]
        + [pl.BlockSpec(memory_space=pltpu.VMEM)] * 3,
        out_specs=pl.BlockSpec(memory_space=pltpu.VMEM),
        scratch_shapes=[pltpu.VMEM((256, 2048), jnp.bfloat16)],
        cost_estimate=cost(2 * 512 * 2048 * (2048 + cols), 10**7),
        compiler_params=pltpu.CompilerParams(**PARAMS),
        name="near_rows",
    )(scalars, gram, *panels)


def place_kernel(far, s_ref, piece, *rest):
    out, sems = rest[-2:]
    matrix = 1 - s_ref[3] if far else s_ref[3]
    copies = [
        pltpu.make_async_copy(piece.at[0], out.at[matrix, :, s_ref[4]], sems.at[0]),
        pltpu.make_async_copy(piece.at[1], out.at[matrix, :, 1 - s_ref[4]], sems.at[1]),
    ]
    for copy in copies:
        copy.start()
    for copy in copies:
        copy.wait()


def place_rows(far, scalars, piece, *into):
    _, groups, rows, cols = piece.shape
    return pl.pallas_call(
        functools.partial(place_kernel, far),
        out_shape=jax.ShapeDtypeStruct((2, groups, 2, rows, cols), jnp.bfloat16),
        in_specs=[pl.BlockSpec(memory_space=pltpu.SMEM)]
        + [pl.BlockSpec(memory_space=pl.ANY)] * (1 + len(into)),
        out_specs=pl.BlockSpec(memory_space=pl.ANY),
        scratch_shapes=[pltpu.SemaphoreType.DMA((2,))],
        input_output_aliases={2: 0} if into else {},
        compiler_params=pltpu.CompilerParams(**PARAMS),
        name="place_rows",
    )(scalars, piece, *into)


def home_far(m, r, c):
    return m, (1 - r // 2) * 2 + c, r % 2


def home_near(m, r, c):
    return m, (r // 2) * 2 + c, r % 2


def fast_body(iterate):
    x = iterate[:, 0]
    mats, rows, cols = x.shape
    m, r, c = (lax.axis_index(axis) for axis in AXES)
    q, b = r // 2, r % 2
    scalars = jnp.stack([2 * m + b, 2 * (1 - q) + c, 2 * q + c, q, b]).astype(jnp.int32)
    pieces = cut(x).reshape(32, rows // 2, cols // CHIPS)
    own = lax.all_to_all(pieces, ("gr", "mat", "gc"), 0, 0, tiled=True)
    own = own.reshape(1024, cols // CHIPS)
    panels = (own, send(own, other_core))
    made = gram_strips(scalars, *panels)
    thirds, others = gather_strips(sum_strips(made[:3], made[3:], 1.0 / cols))
    gram, far = first_rows(scalars, thirds, others, panels)
    far_home = send(far, home_far)
    near_home = send(near_rows(scalars, gram, panels), home_near)
    shape = (2, 8, 32, cols // CHIPS)
    result = place_rows(True, scalars, far_home.reshape(shape))
    result = place_rows(False, scalars, near_home.reshape(shape), result)
    return result.reshape(mats, 512, cols // CHIPS)


def solution(mesh):
    fast = tuple(mesh.shape[axis] for axis in AXES) == (4, 4, 2)
    return jax.shard_map(
        fast_body if fast else plain_body,
        mesh=mesh,
        in_specs=(P(None, "gr", ("mat", "gc"), None),),
        out_specs=P(None, "gr", ("mat", "gc")),
        check_vma=False,
    )
```

```python
import functools

import jax
import jax.numpy as jnp
from jax import lax
from jax.experimental import pallas as pl
from jax.experimental.pallas import tpu as pltpu
from jax.sharding import PartitionSpec as P

linear_coef = 3.4445
cubic_coef = -4.775
quintic_coef = 2.0315

AXES = ("mat", "gr", "gc")


def plain_body(iterate):
    regrouped = lax.all_to_all(iterate, ("mat", "gc"), split_axis=3, concat_axis=2, tiled=True)
    row_block = regrouped[:, 0]
    panel_rows = lax.all_gather(row_block, "gr", axis=1, tiled=True)
    total_rows = panel_rows.shape[1]
    groups = lax.axis_size(("mat", "gc"))
    gram_width = total_rows // groups
    inv_cols = 1.0 / iterate.shape[-1]
    partial_value = jnp.einsum(
        "irc,ijc->irj", row_block, panel_rows, preferred_element_type=jnp.float32
    )
    gram_rows = (lax.psum(partial_value, ("mat", "gc")) * inv_cols).astype(jnp.bfloat16)
    own_block = lax.dynamic_slice_in_dim(
        gram_rows, lax.axis_index(("mat", "gc")) * gram_width, gram_width, 2
    )
    square = jnp.einsum(
        "irk,ikj->irj",
        gram_rows,
        lax.all_gather(own_block, "gr", axis=1, tiled=True),
        preferred_element_type=jnp.float32,
    )
    poly_block = (cubic_coef * own_block.astype(jnp.float32) + quintic_coef * square).astype(
        jnp.bfloat16
    )
    mixed_sum = jnp.einsum(
        "irk,ikc->irc",
        lax.all_gather(poly_block, ("mat", "gc"), axis=2, tiled=True),
        panel_rows,
        preferred_element_type=jnp.float32,
    )
    result = linear_coef * row_block.astype(jnp.float32) + mixed_sum
    return result.astype(jnp.bfloat16)


CHIPS = 8
BLOCK = 128
STRIP = 9 * BLOCK
THIRD = STRIP // 3
ORDERS = ((2, 4, 1), (4, 1, 2), (1, 2, 4))
PARAMS = dict(vmem_limit_bytes=28 * 1024 * 1024)


def cost(flops, bytes_accessed):
    return pl.CostEstimate(flops=flops, bytes_accessed=bytes_accessed, transcendentals=0)


def offset(third, place):
    axes = ORDERS[third]
    return sum(axes[k] for k in range(3) if place >> (2 - k) & 1)


def send(value, move):
    perm = []
    for m in range(4):
        for r in range(4):
            for c in range(2):
                to = move(m, r, c)
                perm.append((m * 8 + r * 2 + c, to[0] * 8 + to[1] * 2 + to[2]))
    return lax.ppermute(value, AXES, perm)


def across(d):
    return lambda m, r, c: (m ^ (d >> 1), r ^ (d & 1), c)


def other_core(m, r, c):
    return m, r, 1 - c


def cut_kernel(x_ref, o_ref, sems):
    copies = []
    width = o_ref.shape[-1]
    for q in range(2):
        for k in range(CHIPS):
            copies.append(
                pltpu.make_async_copy(
                    x_ref.at[q, :, pl.ds(k * width, width)],
                    o_ref.at[q, k % 2, k // 2],
                    sems.at[q * CHIPS + k],
                )
            )
    for copy in copies:
        copy.start()
    for copy in copies:
        copy.wait()


def cut(x):
    _, rows, cols = x.shape
    return pl.pallas_call(
        cut_kernel,
        out_shape=jax.ShapeDtypeStruct((2, 2, 4, rows, cols // CHIPS), x.dtype),
        in_specs=[pl.BlockSpec(memory_space=pl.ANY)],
        out_specs=pl.BlockSpec(memory_space=pl.ANY),
        scratch_shapes=[pltpu.SemaphoreType.DMA((16,))],
        compiler_params=pltpu.CompilerParams(**PARAMS),
        name="cut_columns",
    )(x)


GRAM_DIMS = (((1,), (1,)), ((), ()))


def own_kernel(own, strips, panel, sem):
    copy = pltpu.make_async_copy(own, panel.at[pl.ds(0, 1024)], sem)
    copy.start()
    for t in range(4):
        lo = 256 * t
        made = lax.dot_general(
            own[lo : lo + 256, :], own[lo:, :], GRAM_DIMS, preferred_element_type=jnp.float32
        )
        strips[2 * t, :, : 1024 - lo] = made[:BLOCK]
        strips[2 * t + 1, :, : 1024 - BLOCK - lo] = made[BLOCK:, BLOCK:]
    copy.wait()


def own_strips(own):
    rows, cols = own.shape
    return pl.pallas_call(
        own_kernel,
        out_shape=[
            jax.ShapeDtypeStruct((CHIPS, BLOCK, STRIP), jnp.float32),
            jax.ShapeDtypeStruct((2 * rows, cols), own.dtype),
        ],
        in_specs=[pl.BlockSpec(memory_space=pltpu.VMEM)],
        out_specs=[pl.BlockSpec(memory_space=pltpu.VMEM)] * 2,
        scratch_shapes=[pltpu.SemaphoreType.DMA],
        cost_estimate=cost(1024 * 1280 * cols, 10**7),
        compiler_params=pltpu.CompilerParams(**PARAMS),
        name="own_strips",
    )(own)


def gram_kernel(p_ref, strips_in, panel_in, own, other, *rest):
    del strips_in, panel_in
    keep, away, (strips, panel, sem) = rest[:3], rest[3:6], rest[6:]
    copy = pltpu.make_async_copy(other, panel.at[pl.ds(1024, 1024)], sem)
    copy.start()
    for t in range(4):
        lo = 256 * t
        made = lax.dot_general(
            own[lo : lo + 256, :],
            other[: lo + 256, :],
            GRAM_DIMS,
            preferred_element_type=jnp.float32,
        )
        strips[2 * t, :, 1024 - lo :] = made[:BLOCK, : BLOCK + lo]
        strips[2 * t + 1, :, 1024 - BLOCK - lo :] = made[BLOCK:]
    p = p_ref[0]
    for i in range(3):
        cols = slice(THIRD * i, THIRD * (i + 1))
        for place in range(4):
            keep[i][place] = strips[p ^ offset(i, place), :, cols]
            away[i][place] = strips[p ^ offset(i, place + 4), :, cols].astype(jnp.bfloat16)
    copy.wait()


def gram_strips(p, strips, panel, own, other):
    shape = (4, BLOCK, THIRD)
    made = pl.pallas_call(
        gram_kernel,
        out_shape=[jax.ShapeDtypeStruct(shape, jnp.float32)] * 3
        + [jax.ShapeDtypeStruct(shape, jnp.bfloat16)] * 3
        + [jax.ShapeDtypeStruct(v.shape, v.dtype) for v in (strips, panel)],
        in_specs=[pl.BlockSpec(memory_space=pltpu.SMEM)]
        + [pl.BlockSpec(memory_space=pltpu.VMEM)] * 4,
        out_specs=[pl.BlockSpec(memory_space=pltpu.VMEM)] * 8,
        scratch_shapes=[pltpu.SemaphoreType.DMA],
        input_output_aliases={1: 6, 2: 7},
        cost_estimate=cost(1024 * 1280 * own.shape[-1], 10**7),
        compiler_params=pltpu.CompilerParams(**PARAMS),
        name="gram_strips",
    )(p, strips, panel, own, other)
    return made[:3], made[3:6], made[7]


def halves_kernel(held, came, keep, away):
    half = keep.shape[0]
    total = held[...] + came[...].astype(jnp.float32)
    keep[...] = total[:half]
    away[...] = total[half:].astype(jnp.bfloat16)


def pairs_kernel(held, came, keep, away):
    total = held[...] + came[...].astype(jnp.float32)
    keep[...] = total
    away[0] = total[1].astype(jnp.bfloat16)
    away[1] = total[0].astype(jnp.bfloat16)


def last_kernel(scale, held, came, out):
    total = held[...] + came[...].astype(jnp.float32)
    out[...] = (total * scale).astype(jnp.bfloat16)


def add(kernel, name, types, held, came):
    shape = (2, BLOCK, THIRD)
    return pl.pallas_call(
        kernel,
        out_shape=[jax.ShapeDtypeStruct(shape, dtype) for dtype in types],
        in_specs=[pl.BlockSpec(memory_space=pltpu.VMEM)] * 2,
        out_specs=[pl.BlockSpec(memory_space=pltpu.VMEM)] * len(types),
        cost_estimate=cost(10**5, 10**6),
        compiler_params=pltpu.CompilerParams(**PARAMS),
        name=name,
    )(held, came)


def sum_third(third, keep, away, scale):
    first, second, last = (across(axis) for axis in ORDERS[third])
    both = (jnp.float32, jnp.bfloat16)
    keep, away = add(halves_kernel, "add_halves", both, keep, send(away, first))
    keep, away = add(pairs_kernel, "add_pairs", both, keep, send(away, second))
    (made,) = add(
        functools.partial(last_kernel, scale), "add_last", both[1:], keep, send(away, last)
    )
    return made


def sum_strips(keep, away, scale):
    return [sum_third(third, keep[third], away[third], scale) for third in range(3)]


def gather_strips(parts):
    came = [send(parts[i], across(ORDERS[i][1])) for i in range(3)]
    early = [jnp.concatenate([parts[i], came[i]], axis=0) for i in range(3)]
    late = [send(early[i], across(ORDERS[i][0])) for i in range(3)]
    early += [send(part, other_core) for part in early]
    late += [send(part, other_core) for part in late]
    return early + late


def fill(gram, p, thirds, first_place):
    for k, ref in enumerate(thirds):
        third, far_half = k % 3, 8 * (k // 3)
        for j in range(4):
            row = (p ^ offset(third, first_place + j)) + far_half
            row_at = pl.ds(pl.multiple_of(row * BLOCK, BLOCK), BLOCK)
            for d in range(3 * third, 3 * third + 3):
                col = (row + d) & 15
                col_at = pl.ds(pl.multiple_of(col * BLOCK, BLOCK), BLOCK)
                block = ref[j, :, BLOCK * (d - 3 * third) : BLOCK * (d - 3 * third + 1)]
                gram[row_at, col_at] = block
                if 1 <= d <= 7:
                    gram[col_at, row_at] = block.T


def result_rows(gram, panel, poly, place, half):
    start = pl.multiple_of(1024 * half + place * 256, 256)
    rows = gram[pl.ds(start, 256), :]
    for n in range(0, 2048, 512):
        square = jnp.dot(rows, gram[:, n : n + 512], preferred_element_type=jnp.float32)
        poly[:, n : n + 512] = (
            cubic_coef * rows[:, n : n + 512].astype(jnp.float32) + quintic_coef * square
        ).astype(jnp.bfloat16)
    mixed = jnp.dot(poly[...], panel[...], preferred_element_type=jnp.float32)
    return (linear_coef * panel[pl.ds(start, 256), :].astype(jnp.float32) + mixed).astype(
        jnp.bfloat16
    )


def first_kernel(s_ref, *refs):
    strips, panel, gram, out, poly = refs[:12], *refs[12:]
    fill(gram, s_ref[0], strips[:6], 0)
    fill(gram, s_ref[0], strips[6:], 4)
    for half in range(2):
        out[256 * half : 256 * (half + 1)] = result_rows(gram, panel, poly, s_ref[1], half)


def first_rows(scalars, strips, panel):
    cols = panel.shape[-1]
    return pl.pallas_call(
        first_kernel,
        out_shape=[
            jax.ShapeDtypeStruct((2048, 2048), jnp.bfloat16),
            jax.ShapeDtypeStruct((512, cols), jnp.bfloat16),
        ],
        in_specs=[pl.BlockSpec(memory_space=pltpu.SMEM)]
        + [pl.BlockSpec(memory_space=pltpu.VMEM)] * 13,
        out_specs=[pl.BlockSpec(memory_space=pltpu.VMEM)] * 2,
        scratch_shapes=[pltpu.VMEM((256, 2048), jnp.bfloat16)],
        cost_estimate=cost(2 * 512 * 2048 * (2048 + cols), 3 * 10**7),
        compiler_params=pltpu.CompilerParams(**PARAMS),
        name="first_rows",
    )(scalars, *strips, panel)


def near_kernel(s_ref, gram, panel, out, poly):
    for half in range(2):
        out[256 * half : 256 * (half + 1)] = result_rows(gram, panel, poly, s_ref[2], half)


def near_rows(scalars, gram, panel):
    cols = panel.shape[-1]
    return pl.pallas_call(
        near_kernel,
        out_shape=jax.ShapeDtypeStruct((512, cols), jnp.bfloat16),
        in_specs=[pl.BlockSpec(memory_space=pltpu.SMEM)]
        + [pl.BlockSpec(memory_space=pltpu.VMEM)] * 2,
        out_specs=pl.BlockSpec(memory_space=pltpu.VMEM),
        scratch_shapes=[pltpu.VMEM((256, 2048), jnp.bfloat16)],
        cost_estimate=cost(2 * 512 * 2048 * (2048 + cols), 10**7),
        compiler_params=pltpu.CompilerParams(**PARAMS),
        name="near_rows",
    )(scalars, gram, panel)


def hold_kernel(piece, out):
    del piece, out


def hold(piece):
    return pl.pallas_call(
        hold_kernel,
        out_shape=jax.ShapeDtypeStruct(piece.shape, piece.dtype),
        in_specs=[pl.BlockSpec(memory_space=pl.ANY)],
        out_specs=pl.BlockSpec(memory_space=pl.ANY),
        input_output_aliases={0: 0},
        cost_estimate=cost(2 * 10**10, 10**6),
        compiler_params=pltpu.CompilerParams(**PARAMS),
        name="hold",
    )(piece)


def place_kernel(s_ref, near, far, out, sems):
    matrix, core = s_ref[3], s_ref[4]
    copies = []
    for piece, i in ((near, matrix), (far, 1 - matrix)):
        for half, sub in enumerate((core, 1 - core)):
            sem = sems.at[len(copies)]
            copies.append(pltpu.make_async_copy(piece.at[half], out.at[i, :, sub], sem))
    for copy in copies:
        copy.start()
    for copy in copies:
        copy.wait()


def place_rows(scalars, near, far):
    _, groups, rows, cols = near.shape
    return pl.pallas_call(
        place_kernel,
        out_shape=jax.ShapeDtypeStruct((2, groups, 2, rows, cols), jnp.bfloat16),
        in_specs=[pl.BlockSpec(memory_space=pltpu.SMEM)]
        + [pl.BlockSpec(memory_space=pl.ANY)] * 2,
        out_specs=pl.BlockSpec(memory_space=pl.ANY),
        scratch_shapes=[pltpu.SemaphoreType.DMA((4,))],
        compiler_params=pltpu.CompilerParams(**PARAMS),
        name="place_rows",
    )(scalars, near, far)


def home_far(m, r, c):
    return m, (1 - r // 2) * 2 + c, r % 2


def home_near(m, r, c):
    return m, (r // 2) * 2 + c, r % 2


def fast_body(iterate):
    x = iterate[:, 0]
    mats, rows, cols = x.shape
    m, r, c = (lax.axis_index(axis) for axis in AXES)
    q, b = r // 2, r % 2
    scalars = jnp.stack([2 * m + b, 2 * (1 - q) + c, 2 * q + c, q, b]).astype(jnp.int32)
    pieces = cut(x).reshape(32, rows // 2, cols // CHIPS)
    own = lax.all_to_all(pieces, ("gr", "mat", "gc"), 0, 0, tiled=True)
    own = own.reshape(1024, cols // CHIPS)
    other = send(own, other_core)
    keep, away, panel = gram_strips(scalars, *own_strips(own), own, other)
    strips = gather_strips(sum_strips(keep, away, 1.0 / cols))
    gram, far = first_rows(scalars, strips, panel)
    far = hold(send(far, home_far))
    near = send(near_rows(scalars, gram, panel), home_near)
    shape = (2, 8, 32, cols // CHIPS)
    result = place_rows(scalars, near.reshape(shape), far.reshape(shape))
    return result.reshape(mats, 512, cols // CHIPS)


def solution(mesh):
    fast = tuple(mesh.shape[axis] for axis in AXES) == (4, 4, 2)
    return jax.shard_map(
        fast_body if fast else plain_body,
        mesh=mesh,
        in_specs=(P(None, "gr", ("mat", "gc"), None),),
        out_specs=P(None, "gr", ("mat", "gc")),
        check_vma=False,
    )
```

```python
import functools

import jax
import jax.numpy as jnp
from jax import lax
from jax.experimental import pallas as pl
from jax.experimental.pallas import tpu as pltpu
from jax.sharding import PartitionSpec as P

linear_coef = 3.4445
cubic_coef = -4.775
quintic_coef = 2.0315

AXES = ("mat", "gr", "gc")


def plain_body(iterate):
    regrouped = lax.all_to_all(iterate, ("mat", "gc"), split_axis=3, concat_axis=2, tiled=True)
    row_block = regrouped[:, 0]
    panel_rows = lax.all_gather(row_block, "gr", axis=1, tiled=True)
    total_rows = panel_rows.shape[1]
    groups = lax.axis_size(("mat", "gc"))
    gram_width = total_rows // groups
    inv_cols = 1.0 / iterate.shape[-1]
    partial_value = jnp.einsum(
        "irc,ijc->irj", row_block, panel_rows, preferred_element_type=jnp.float32
    )
    gram_rows = (lax.psum(partial_value, ("mat", "gc")) * inv_cols).astype(jnp.bfloat16)
    own_block = lax.dynamic_slice_in_dim(
        gram_rows, lax.axis_index(("mat", "gc")) * gram_width, gram_width, 2
    )
    square = jnp.einsum(
        "irk,ikj->irj",
        gram_rows,
        lax.all_gather(own_block, "gr", axis=1, tiled=True),
        preferred_element_type=jnp.float32,
    )
    poly_block = (cubic_coef * own_block.astype(jnp.float32) + quintic_coef * square).astype(
        jnp.bfloat16
    )
    mixed_sum = jnp.einsum(
        "irk,ikc->irc",
        lax.all_gather(poly_block, ("mat", "gc"), axis=2, tiled=True),
        panel_rows,
        preferred_element_type=jnp.float32,
    )
    result = linear_coef * row_block.astype(jnp.float32) + mixed_sum
    return result.astype(jnp.bfloat16)


CHIPS = 8
BLOCK = 128
STRIP = 9 * BLOCK
THIRD = STRIP // 3
ORDERS = ((2, 4, 1), (4, 1, 2), (1, 2, 4))
PARAMS = dict(vmem_limit_bytes=28 * 1024 * 1024)


def cost(flops, bytes_accessed):
    return pl.CostEstimate(flops=flops, bytes_accessed=bytes_accessed, transcendentals=0)


def offset(third, place):
    axes = ORDERS[third]
    return sum(axes[k] for k in range(3) if place >> (2 - k) & 1)


def send(value, move):
    perm = []
    for m in range(4):
        for r in range(4):
            for c in range(2):
                to = move(m, r, c)
                perm.append((m * 8 + r * 2 + c, to[0] * 8 + to[1] * 2 + to[2]))
    return lax.ppermute(value, AXES, perm)


def across(d):
    return lambda m, r, c: (m ^ (d >> 1), r ^ (d & 1), c)


def other_core(m, r, c):
    return m, r, 1 - c


def cut_kernel(x_ref, o_ref, sems):
    copies = []
    width = o_ref.shape[-1]
    for q in range(2):
        for k in range(CHIPS):
            copies.append(
                pltpu.make_async_copy(
                    x_ref.at[q, :, pl.ds(k * width, width)],
                    o_ref.at[q, k % 2, k // 2],
                    sems.at[q * CHIPS + k],
                )
            )
    for copy in copies:
        copy.start()
    for copy in copies:
        copy.wait()


def cut(x):
    _, rows, cols = x.shape
    return pl.pallas_call(
        cut_kernel,
        out_shape=jax.ShapeDtypeStruct((2, 2, 4, rows, cols // CHIPS), x.dtype),
        in_specs=[pl.BlockSpec(memory_space=pl.ANY)],
        out_specs=pl.BlockSpec(memory_space=pl.ANY),
        scratch_shapes=[pltpu.SemaphoreType.DMA((16,))],
        compiler_params=pltpu.CompilerParams(**PARAMS),
        name="cut_columns",
    )(x)


GRAM_DIMS = (((1,), (1,)), ((), ()))


def own_kernel(own, strips, panel, sem):
    copy = pltpu.make_async_copy(own, panel.at[pl.ds(0, 1024)], sem)
    copy.start()
    for t in range(4):
        lo = 256 * t
        made = lax.dot_general(
            own[lo : lo + 256, :], own[lo:, :], GRAM_DIMS, preferred_element_type=jnp.float32
        )
        strips[2 * t, :, : 1024 - lo] = made[:BLOCK]
        strips[2 * t + 1, :, : 1024 - BLOCK - lo] = made[BLOCK:, BLOCK:]
    copy.wait()


def own_strips(own):
    rows, cols = own.shape
    return pl.pallas_call(
        own_kernel,
        out_shape=[
            jax.ShapeDtypeStruct((CHIPS, BLOCK, STRIP), jnp.float32),
            jax.ShapeDtypeStruct((2 * rows, cols), own.dtype),
        ],
        in_specs=[pl.BlockSpec(memory_space=pltpu.VMEM)],
        out_specs=[pl.BlockSpec(memory_space=pltpu.VMEM)] * 2,
        scratch_shapes=[pltpu.SemaphoreType.DMA],
        cost_estimate=cost(1024 * 1280 * cols, 10**7),
        compiler_params=pltpu.CompilerParams(**PARAMS),
        name="own_strips",
    )(own)


def gram_kernel(p_ref, strips_in, panel_in, own, other, *rest):
    del strips_in, panel_in
    keep, away, (strips, panel, sem) = rest[:3], rest[3:6], rest[6:]
    copy = pltpu.make_async_copy(other, panel.at[pl.ds(1024, 1024)], sem)
    copy.start()
    for t in range(4):
        lo = 256 * t
        made = lax.dot_general(
            own[lo : lo + 256, :],
            other[: lo + 256, :],
            GRAM_DIMS,
            preferred_element_type=jnp.float32,
        )
        strips[2 * t, :, 1024 - lo :] = made[:BLOCK, : BLOCK + lo]
        strips[2 * t + 1, :, 1024 - BLOCK - lo :] = made[BLOCK:]
    p = p_ref[0]
    for i in range(3):
        cols = slice(THIRD * i, THIRD * (i + 1))
        for place in range(4):
            keep[i][place] = strips[p ^ offset(i, place), :, cols]
            away[i][place] = strips[p ^ offset(i, place + 4), :, cols].astype(jnp.bfloat16)
    copy.wait()


def gram_strips(p, strips, panel, own, other):
    shape = (4, BLOCK, THIRD)
    made = pl.pallas_call(
        gram_kernel,
        out_shape=[jax.ShapeDtypeStruct(shape, jnp.float32)] * 3
        + [jax.ShapeDtypeStruct(shape, jnp.bfloat16)] * 3
        + [jax.ShapeDtypeStruct(v.shape, v.dtype) for v in (strips, panel)],
        in_specs=[pl.BlockSpec(memory_space=pltpu.SMEM)]
        + [pl.BlockSpec(memory_space=pltpu.VMEM)] * 4,
        out_specs=[pl.BlockSpec(memory_space=pltpu.VMEM)] * 8,
        scratch_shapes=[pltpu.SemaphoreType.DMA],
        input_output_aliases={1: 6, 2: 7},
        cost_estimate=cost(1024 * 1280 * own.shape[-1], 10**7),
        compiler_params=pltpu.CompilerParams(**PARAMS),
        name="gram_strips",
    )(p, strips, panel, own, other)
    return made[:3], made[3:6], made[7]


def halves_kernel(held, came, keep, away):
    half = keep.shape[0]
    total = held[...] + came[...].astype(jnp.float32)
    keep[...] = total[:half]
    away[...] = total[half:].astype(jnp.bfloat16)


def pairs_kernel(held, came, keep, away):
    total = held[...] + came[...].astype(jnp.float32)
    keep[...] = total
    away[0] = total[1].astype(jnp.bfloat16)
    away[1] = total[0].astype(jnp.bfloat16)


def last_kernel(scale, held, came, out):
    total = held[...] + came[...].astype(jnp.float32)
    out[...] = (total * scale).astype(jnp.bfloat16)


def add(kernel, name, types, held, came):
    shape = (2, BLOCK, THIRD)
    return pl.pallas_call(
        kernel,
        out_shape=[jax.ShapeDtypeStruct(shape, dtype) for dtype in types],
        in_specs=[pl.BlockSpec(memory_space=pltpu.VMEM)] * 2,
        out_specs=[pl.BlockSpec(memory_space=pltpu.VMEM)] * len(types),
        cost_estimate=cost(10**5, 10**6),
        compiler_params=pltpu.CompilerParams(**PARAMS),
        name=name,
    )(held, came)


def sum_third(third, keep, away, scale):
    first, second, last = (across(axis) for axis in ORDERS[third])
    both = (jnp.float32, jnp.bfloat16)
    keep, away = add(halves_kernel, "add_halves", both, keep, send(away, first))
    keep, away = add(pairs_kernel, "add_pairs", both, keep, send(away, second))
    (made,) = add(
        functools.partial(last_kernel, scale), "add_last", both[1:], keep, send(away, last)
    )
    return made


def sum_strips(keep, away, scale):
    return [sum_third(third, keep[third], away[third], scale) for third in range(3)]


def gather_strips(parts):
    came = [send(parts[i], across(ORDERS[i][1])) for i in range(3)]
    early = [jnp.concatenate([parts[i], came[i]], axis=0) for i in range(3)]
    late = [send(early[i], across(ORDERS[i][0])) for i in range(3)]
    early += [send(part, other_core) for part in early]
    late += [send(part, other_core) for part in late]
    return early + late


def fill(gram, p, thirds, first_place):
    for k, ref in enumerate(thirds):
        third, far_half = k % 3, 8 * (k // 3)
        for j in range(4):
            row = (p ^ offset(third, first_place + j)) + far_half
            row_at = pl.ds(pl.multiple_of(row * BLOCK, BLOCK), BLOCK)
            for d in range(3 * third, 3 * third + 3):
                col = (row + d) & 15
                col_at = pl.ds(pl.multiple_of(col * BLOCK, BLOCK), BLOCK)
                block = ref[j, :, BLOCK * (d - 3 * third) : BLOCK * (d - 3 * third + 1)]
                gram[row_at, col_at] = block
                if 1 <= d <= 7:
                    gram[col_at, row_at] = block.T


def result_rows(gram, panel, poly, place, half, first, count):
    start = pl.multiple_of(1024 * half + place * 256 + first, BLOCK)
    rows = gram[pl.ds(start, count), :]
    for n in range(0, 2048, 512):
        square = jnp.dot(rows, gram[:, n : n + 512], preferred_element_type=jnp.float32)
        poly[:count, n : n + 512] = (
            cubic_coef * rows[:, n : n + 512].astype(jnp.float32) + quintic_coef * square
        ).astype(jnp.bfloat16)
    mixed = jnp.dot(poly[:count], panel[...], preferred_element_type=jnp.float32)
    return (linear_coef * panel[pl.ds(start, count), :].astype(jnp.float32) + mixed).astype(
        jnp.bfloat16
    )


def first_kernel(s_ref, *refs):
    strips, panel, gram, out, poly = refs[:12], *refs[12:]
    fill(gram, s_ref[0], strips[:6], 0)
    fill(gram, s_ref[0], strips[6:], 4)
    out[:256] = result_rows(gram, panel, poly, s_ref[1], 0, 0, 256)
    out[256:] = result_rows(gram, panel, poly, s_ref[1], 1, 0, 128)


def first_rows(scalars, strips, panel):
    cols = panel.shape[-1]
    return pl.pallas_call(
        first_kernel,
        out_shape=[
            jax.ShapeDtypeStruct((2048, 2048), jnp.bfloat16),
            jax.ShapeDtypeStruct((384, cols), jnp.bfloat16),
        ],
        in_specs=[pl.BlockSpec(memory_space=pltpu.SMEM)]
        + [pl.BlockSpec(memory_space=pltpu.VMEM)] * 13,
        out_specs=[pl.BlockSpec(memory_space=pltpu.VMEM)] * 2,
        scratch_shapes=[pltpu.VMEM((256, 2048), jnp.bfloat16)],
        cost_estimate=cost(2 * 384 * 2048 * (2048 + cols), 3 * 10**7),
        compiler_params=pltpu.CompilerParams(**PARAMS),
        name="first_rows",
    )(scalars, *strips, panel)


def more_kernel(scalar, parts, s_ref, gram, panel, *rest):
    outs, poly = rest[:-1], rest[-1]
    for part, out in zip(parts, outs, strict=True):
        out[...] = result_rows(gram, panel, poly, s_ref[scalar], *part)


def more_rows(scalar, parts, scalars, gram, panel):
    cols = panel.shape[-1]
    rows = sum(part[2] for part in parts)
    return pl.pallas_call(
        functools.partial(more_kernel, scalar, parts),
        out_shape=[jax.ShapeDtypeStruct((part[2], cols), jnp.bfloat16) for part in parts],
        in_specs=[pl.BlockSpec(memory_space=pltpu.SMEM)]
        + [pl.BlockSpec(memory_space=pltpu.VMEM)] * 2,
        out_specs=[pl.BlockSpec(memory_space=pltpu.VMEM)] * len(parts),
        scratch_shapes=[pltpu.VMEM((256, 2048), jnp.bfloat16)],
        cost_estimate=cost(2 * rows * 2048 * (2048 + cols), 10**7),
        compiler_params=pltpu.CompilerParams(**PARAMS),
        name="more_rows",
    )(scalars, gram, panel)


def hold_kernel(*refs):
    del refs


def hold(bytes_moved, piece, *earlier):
    return pl.pallas_call(
        hold_kernel,
        out_shape=jax.ShapeDtypeStruct(piece.shape, piece.dtype),
        in_specs=[pl.BlockSpec(memory_space=pl.ANY)] * (1 + len(earlier)),
        out_specs=pl.BlockSpec(memory_space=pl.ANY),
        input_output_aliases={0: 0},
        cost_estimate=cost(10**6, bytes_moved),
        compiler_params=pltpu.CompilerParams(**PARAMS),
        name="hold",
    )(piece, *earlier)


def place_kernel(s_ref, far_first, far_second, near_own, near_other, out, sems):
    matrix, core = s_ref[3], s_ref[4]
    moves = (
        (far_first.at[0:8], out.at[1 - matrix, :, core]),
        (far_first.at[8:12], out.at[1 - matrix, 0:4, 1 - core]),
        (far_second, out.at[1 - matrix, 4:8, 1 - core]),
        (near_own, out.at[matrix, :, core]),
        (near_other, out.at[matrix, :, 1 - core]),
    )
    copies = [
        pltpu.make_async_copy(source, target, sems.at[k])
        for k, (source, target) in enumerate(moves)
    ]
    for copy in copies:
        copy.start()
    for copy in copies:
        copy.wait()


def place_rows(scalars, *pieces):
    _, rows, cols = pieces[0].shape
    return pl.pallas_call(
        place_kernel,
        out_shape=jax.ShapeDtypeStruct((2, 8, 2, rows, cols), jnp.bfloat16),
        in_specs=[pl.BlockSpec(memory_space=pltpu.SMEM)]
        + [pl.BlockSpec(memory_space=pl.ANY)] * len(pieces),
        out_specs=pl.BlockSpec(memory_space=pl.ANY),
        scratch_shapes=[pltpu.SemaphoreType.DMA((5,))],
        compiler_params=pltpu.CompilerParams(**PARAMS),
        name="place_rows",
    )(scalars, *pieces)


def home_far(m, r, c):
    return m, (1 - r // 2) * 2 + c, r % 2


def home_near(m, r, c):
    return m, (r // 2) * 2 + c, r % 2


def fast_body(iterate):
    x = iterate[:, 0]
    mats, rows, cols = x.shape
    m, r, c = (lax.axis_index(axis) for axis in AXES)
    q, b = r // 2, r % 2
    scalars = jnp.stack([2 * m + b, 2 * (1 - q) + c, 2 * q + c, q, b]).astype(jnp.int32)
    pieces = cut(x).reshape(32, rows // 2, cols // CHIPS)
    own = lax.all_to_all(pieces, ("gr", "mat", "gc"), 0, 0, tiled=True)
    own = own.reshape(1024, cols // CHIPS)
    other = send(own, other_core)
    keep, away, panel = gram_strips(scalars, *own_strips(own), own, other)
    strips = gather_strips(sum_strips(keep, away, 1.0 / cols))
    gram, far_first = first_rows(scalars, strips, panel)
    far_first = hold(4 * 10**7, send(far_first, home_far))
    (far_second,) = more_rows(1, ((1, 128, 128),), scalars, gram, panel)
    far_second = hold(10**7, send(far_second, home_far))
    near = more_rows(2, ((0, 0, 256), (1, 0, 256)), scalars, gram, panel)
    near = [send(piece, home_near) for piece in near]
    pieces = [v.reshape(-1, 32, cols // CHIPS) for v in (far_first, far_second, *near)]
    return place_rows(scalars, *pieces).reshape(mats, 512, cols // CHIPS)


def solution(mesh):
    fast = tuple(mesh.shape[axis] for axis in AXES) == (4, 4, 2)
    return jax.shard_map(
        fast_body if fast else plain_body,
        mesh=mesh,
        in_specs=(P(None, "gr", ("mat", "gc"), None),),
        out_specs=P(None, "gr", ("mat", "gc")),
        check_vma=False,
    )
```

```python
import functools

import jax
import jax.numpy as jnp
from jax import lax
from jax.experimental import pallas as pl
from jax.experimental.pallas import tpu as pltpu
from jax.sharding import PartitionSpec as P

linear_coef = 3.4445
cubic_coef = -4.775
quintic_coef = 2.0315

AXES = ("mat", "gr", "gc")


def plain_body(iterate):
    regrouped = lax.all_to_all(iterate, ("mat", "gc"), split_axis=3, concat_axis=2, tiled=True)
    row_block = regrouped[:, 0]
    panel_rows = lax.all_gather(row_block, "gr", axis=1, tiled=True)
    total_rows = panel_rows.shape[1]
    groups = lax.axis_size(("mat", "gc"))
    gram_width = total_rows // groups
    inv_cols = 1.0 / iterate.shape[-1]
    partial_value = jnp.einsum(
        "irc,ijc->irj", row_block, panel_rows, preferred_element_type=jnp.float32
    )
    gram_rows = (lax.psum(partial_value, ("mat", "gc")) * inv_cols).astype(jnp.bfloat16)
    own_block = lax.dynamic_slice_in_dim(
        gram_rows, lax.axis_index(("mat", "gc")) * gram_width, gram_width, 2
    )
    square = jnp.einsum(
        "irk,ikj->irj",
        gram_rows,
        lax.all_gather(own_block, "gr", axis=1, tiled=True),
        preferred_element_type=jnp.float32,
    )
    poly_block = (cubic_coef * own_block.astype(jnp.float32) + quintic_coef * square).astype(
        jnp.bfloat16
    )
    mixed_sum = jnp.einsum(
        "irk,ikc->irc",
        lax.all_gather(poly_block, ("mat", "gc"), axis=2, tiled=True),
        panel_rows,
        preferred_element_type=jnp.float32,
    )
    result = linear_coef * row_block.astype(jnp.float32) + mixed_sum
    return result.astype(jnp.bfloat16)


CHIPS = 8
BLOCK = 128
STRIP = 9 * BLOCK
THIRD = STRIP // 3
ORDERS = ((2, 4, 1), (4, 1, 2), (1, 2, 4))
PARAMS = dict(vmem_limit_bytes=28 * 1024 * 1024)


def cost(flops, bytes_accessed):
    return pl.CostEstimate(flops=flops, bytes_accessed=bytes_accessed, transcendentals=0)


def offset(third, place):
    axes = ORDERS[third]
    return sum(axes[k] for k in range(3) if place >> (2 - k) & 1)


def send(value, move):
    perm = []
    for m in range(4):
        for r in range(4):
            for c in range(2):
                to = move(m, r, c)
                perm.append((m * 8 + r * 2 + c, to[0] * 8 + to[1] * 2 + to[2]))
    return lax.ppermute(value, AXES, perm)


def across(d):
    return lambda m, r, c: (m ^ (d >> 1), r ^ (d & 1), c)


def other_core(m, r, c):
    return m, r, 1 - c


def cut_kernel(x_ref, o_ref, sems):
    copies = []
    width = o_ref.shape[-1]
    for q in range(2):
        for k in range(CHIPS):
            copies.append(
                pltpu.make_async_copy(
                    x_ref.at[q, :, pl.ds(k * width, width)],
                    o_ref.at[q, k % 2, k // 2],
                    sems.at[q * CHIPS + k],
                )
            )
    for copy in copies:
        copy.start()
    for copy in copies:
        copy.wait()


def cut(x):
    _, rows, cols = x.shape
    return pl.pallas_call(
        cut_kernel,
        out_shape=jax.ShapeDtypeStruct((2, 2, 4, rows, cols // CHIPS), x.dtype),
        in_specs=[pl.BlockSpec(memory_space=pl.ANY)],
        out_specs=pl.BlockSpec(memory_space=pl.ANY),
        scratch_shapes=[pltpu.SemaphoreType.DMA((16,))],
        compiler_params=pltpu.CompilerParams(**PARAMS),
        name="cut_columns",
    )(x)


GRAM_DIMS = (((1,), (1,)), ((), ()))


def own_kernel(own, strips, panel, sem):
    copy = pltpu.make_async_copy(own, panel.at[pl.ds(0, 1024)], sem)
    copy.start()
    for t in range(4):
        lo = 256 * t
        made = lax.dot_general(
            own[lo : lo + 256, :], own[lo:, :], GRAM_DIMS, preferred_element_type=jnp.float32
        )
        strips[2 * t, :, : 1024 - lo] = made[:BLOCK]
        strips[2 * t + 1, :, : 1024 - BLOCK - lo] = made[BLOCK:, BLOCK:]
    copy.wait()


def own_strips(own):
    rows, cols = own.shape
    return pl.pallas_call(
        own_kernel,
        out_shape=[
            jax.ShapeDtypeStruct((CHIPS, BLOCK, STRIP), jnp.float32),
            jax.ShapeDtypeStruct((2 * rows, cols), own.dtype),
        ],
        in_specs=[pl.BlockSpec(memory_space=pltpu.VMEM)],
        out_specs=[pl.BlockSpec(memory_space=pltpu.VMEM)] * 2,
        scratch_shapes=[pltpu.SemaphoreType.DMA],
        cost_estimate=cost(1024 * 1280 * cols, 10**7),
        compiler_params=pltpu.CompilerParams(**PARAMS),
        name="own_strips",
    )(own)


def gram_kernel(p_ref, strips_in, panel_in, own, other, *rest):
    del strips_in, panel_in
    keep, away, (strips, panel, sem) = rest[:3], rest[3:6], rest[6:]
    copy = pltpu.make_async_copy(other, panel.at[pl.ds(1024, 1024)], sem)
    copy.start()
    for t in range(4):
        lo = 256 * t
        made = lax.dot_general(
            own[lo : lo + 256, :],
            other[: lo + 256, :],
            GRAM_DIMS,
            preferred_element_type=jnp.float32,
        )
        strips[2 * t, :, 1024 - lo :] = made[:BLOCK, : BLOCK + lo]
        strips[2 * t + 1, :, 1024 - BLOCK - lo :] = made[BLOCK:]
    p = p_ref[0]
    for i in range(3):
        cols = slice(THIRD * i, THIRD * (i + 1))
        for place in range(4):
            keep[i][place] = strips[p ^ offset(i, place), :, cols]
            away[i][place] = strips[p ^ offset(i, place + 4), :, cols].astype(jnp.bfloat16)
    copy.wait()


def gram_strips(p, strips, panel, own, other):
    shape = (4, BLOCK, THIRD)
    made = pl.pallas_call(
        gram_kernel,
        out_shape=[jax.ShapeDtypeStruct(shape, jnp.float32)] * 3
        + [jax.ShapeDtypeStruct(shape, jnp.bfloat16)] * 3
        + [jax.ShapeDtypeStruct(v.shape, v.dtype) for v in (strips, panel)],
        in_specs=[pl.BlockSpec(memory_space=pltpu.SMEM)]
        + [pl.BlockSpec(memory_space=pltpu.VMEM)] * 4,
        out_specs=[pl.BlockSpec(memory_space=pltpu.VMEM)] * 8,
        scratch_shapes=[pltpu.SemaphoreType.DMA],
        input_output_aliases={1: 6, 2: 7},
        cost_estimate=cost(1024 * 1280 * own.shape[-1], 10**7),
        compiler_params=pltpu.CompilerParams(**PARAMS),
        name="gram_strips",
    )(p, strips, panel, own, other)
    return made[:3], made[3:6], made[7]


def halves_kernel(held, came, keep, away):
    half = keep.shape[0]
    total = held[...] + came[...].astype(jnp.float32)
    keep[...] = total[:half]
    away[...] = total[half:].astype(jnp.bfloat16)


def pairs_kernel(held, came, keep, away):
    total = held[...] + came[...].astype(jnp.float32)
    keep[...] = total
    away[0] = total[1].astype(jnp.bfloat16)
    away[1] = total[0].astype(jnp.bfloat16)


def last_kernel(scale, held, came, out):
    total = held[...] + came[...].astype(jnp.float32)
    out[...] = (total * scale).astype(jnp.bfloat16)


def add(kernel, name, types, held, came):
    shape = (2, BLOCK, THIRD)
    return pl.pallas_call(
        kernel,
        out_shape=[jax.ShapeDtypeStruct(shape, dtype) for dtype in types],
        in_specs=[pl.BlockSpec(memory_space=pltpu.VMEM)] * 2,
        out_specs=[pl.BlockSpec(memory_space=pltpu.VMEM)] * len(types),
        cost_estimate=cost(10**5, 10**6),
        compiler_params=pltpu.CompilerParams(**PARAMS),
        name=name,
    )(held, came)


def sum_third(third, keep, away, scale):
    first, second, last = (across(axis) for axis in ORDERS[third])
    both = (jnp.float32, jnp.bfloat16)
    keep, away = add(halves_kernel, "add_halves", both, keep, send(away, first))
    keep, away = add(pairs_kernel, "add_pairs", both, keep, send(away, second))
    (made,) = add(
        functools.partial(last_kernel, scale), "add_last", both[1:], keep, send(away, last)
    )
    return made


def sum_strips(keep, away, scale):
    return [sum_third(third, keep[third], away[third], scale) for third in range(3)]


def gather_strips(scalars, parts):
    came = [send(parts[i], across(ORDERS[i][1])) for i in range(3)]
    early = [jnp.concatenate([parts[i], came[i]], axis=0) for i in range(3)]
    late = [send(early[i], across(ORDERS[i][0])) for i in range(3)]
    early += [send(part, other_core) for part in early]
    gram = early_gram(scalars, early, late[0])
    return gram, late + [send(part, other_core) for part in late]


def fill(gram, p, thirds, first_place):
    for k, ref in enumerate(thirds):
        third, far_half = k % 3, 8 * (k // 3)
        for j in range(4):
            row = (p ^ offset(third, first_place + j)) + far_half
            row_at = pl.ds(pl.multiple_of(row * BLOCK, BLOCK), BLOCK)
            for d in range(3 * third, 3 * third + 3):
                col = (row + d) & 15
                col_at = pl.ds(pl.multiple_of(col * BLOCK, BLOCK), BLOCK)
                block = ref[j, :, BLOCK * (d - 3 * third) : BLOCK * (d - 3 * third + 1)]
                gram[row_at, col_at] = block
                if 1 <= d <= 7:
                    gram[col_at, row_at] = block.T


def early_kernel(s_ref, *refs):
    fill(refs[7], s_ref[0], refs[:6], 0)


def early_gram(scalars, early, first_late):
    return pl.pallas_call(
        early_kernel,
        out_shape=jax.ShapeDtypeStruct((2048, 2048), jnp.bfloat16),
        in_specs=[pl.BlockSpec(memory_space=pltpu.SMEM)]
        + [pl.BlockSpec(memory_space=pltpu.VMEM)] * 6
        + [pl.BlockSpec(memory_space=pl.ANY)],
        out_specs=pl.BlockSpec(memory_space=pltpu.VMEM),
        cost_estimate=cost(10**5, 3 * 10**7),
        compiler_params=pltpu.CompilerParams(**PARAMS),
        name="early_gram",
    )(scalars, *early, first_late)


def result_rows(gram, panel, poly, place, half, first, count):
    start = pl.multiple_of(1024 * half + place * 256 + first, BLOCK)
    rows = gram[pl.ds(start, count), :]
    for n in range(0, 2048, 512):
        square = jnp.dot(rows, gram[:, n : n + 512], preferred_element_type=jnp.float32)
        poly[:count, n : n + 512] = (
            cubic_coef * rows[:, n : n + 512].astype(jnp.float32) + quintic_coef * square
        ).astype(jnp.bfloat16)
    mixed = jnp.dot(poly[:count], panel[...], preferred_element_type=jnp.float32)
    return (linear_coef * panel[pl.ds(start, count), :].astype(jnp.float32) + mixed).astype(
        jnp.bfloat16
    )


def first_kernel(s_ref, *refs):
    late, gram_in, panel, gram, out, poly = refs[:6], *refs[6:]
    del gram_in
    fill(gram, s_ref[0], late, 4)
    out[:256] = result_rows(gram, panel, poly, s_ref[1], 0, 0, 256)
    out[256:] = result_rows(gram, panel, poly, s_ref[1], 1, 0, 128)


def first_rows(scalars, gram, late, panel):
    cols = panel.shape[-1]
    return pl.pallas_call(
        first_kernel,
        out_shape=[
            jax.ShapeDtypeStruct((2048, 2048), jnp.bfloat16),
            jax.ShapeDtypeStruct((384, cols), jnp.bfloat16),
        ],
        in_specs=[pl.BlockSpec(memory_space=pltpu.SMEM)]
        + [pl.BlockSpec(memory_space=pltpu.VMEM)] * 8,
        out_specs=[pl.BlockSpec(memory_space=pltpu.VMEM)] * 2,
        scratch_shapes=[pltpu.VMEM((256, 2048), jnp.bfloat16)],
        input_output_aliases={7: 0},
        cost_estimate=cost(2 * 384 * 2048 * (2048 + cols), 3 * 10**7),
        compiler_params=pltpu.CompilerParams(**PARAMS),
        name="first_rows",
    )(scalars, *late, gram, panel)


def more_kernel(scalar, parts, s_ref, gram, panel, *rest):
    outs, poly = rest[:-1], rest[-1]
    for part, out in zip(parts, outs, strict=True):
        out[...] = result_rows(gram, panel, poly, s_ref[scalar], *part)


def more_rows(scalar, parts, scalars, gram, panel):
    cols = panel.shape[-1]
    rows = sum(part[2] for part in parts)
    return pl.pallas_call(
        functools.partial(more_kernel, scalar, parts),
        out_shape=[jax.ShapeDtypeStruct((part[2], cols), jnp.bfloat16) for part in parts],
        in_specs=[pl.BlockSpec(memory_space=pltpu.SMEM)]
        + [pl.BlockSpec(memory_space=pltpu.VMEM)] * 2,
        out_specs=[pl.BlockSpec(memory_space=pltpu.VMEM)] * len(parts),
        scratch_shapes=[pltpu.VMEM((256, 2048), jnp.bfloat16)],
        cost_estimate=cost(2 * rows * 2048 * (2048 + cols), 10**7),
        compiler_params=pltpu.CompilerParams(**PARAMS),
        name="more_rows",
    )(scalars, gram, panel)


def hold_kernel(*refs):
    del refs


def hold(bytes_moved, piece, *earlier):
    return pl.pallas_call(
        hold_kernel,
        out_shape=jax.ShapeDtypeStruct(piece.shape, piece.dtype),
        in_specs=[pl.BlockSpec(memory_space=pl.ANY)] * (1 + len(earlier)),
        out_specs=pl.BlockSpec(memory_space=pl.ANY),
        input_output_aliases={0: 0},
        cost_estimate=cost(10**6, bytes_moved),
        compiler_params=pltpu.CompilerParams(**PARAMS),
        name="hold",
    )(piece, *earlier)


def place_kernel(s_ref, far_first, far_second, near_own, near_other, out, sems):
    matrix, core = s_ref[3], s_ref[4]
    moves = (
        (far_first.at[0:8], out.at[1 - matrix, :, core]),
        (far_first.at[8:12], out.at[1 - matrix, 0:4, 1 - core]),
        (far_second, out.at[1 - matrix, 4:8, 1 - core]),
        (near_own, out.at[matrix, :, core]),
        (near_other, out.at[matrix, :, 1 - core]),
    )
    copies = [
        pltpu.make_async_copy(source, target, sems.at[k])
        for k, (source, target) in enumerate(moves)
    ]
    for copy in copies:
        copy.start()
    for copy in copies:
        copy.wait()


def place_rows(scalars, *pieces):
    _, rows, cols = pieces[0].shape
    return pl.pallas_call(
        place_kernel,
        out_shape=jax.ShapeDtypeStruct((2, 8, 2, rows, cols), jnp.bfloat16),
        in_specs=[pl.BlockSpec(memory_space=pltpu.SMEM)]
        + [pl.BlockSpec(memory_space=pl.ANY)] * len(pieces),
        out_specs=pl.BlockSpec(memory_space=pl.ANY),
        scratch_shapes=[pltpu.SemaphoreType.DMA((5,))],
        compiler_params=pltpu.CompilerParams(**PARAMS),
        name="place_rows",
    )(scalars, *pieces)


def home_far(m, r, c):
    return m, (1 - r // 2) * 2 + c, r % 2


def home_near(m, r, c):
    return m, (r // 2) * 2 + c, r % 2


def fast_body(iterate):
    x = iterate[:, 0]
    mats, rows, cols = x.shape
    m, r, c = (lax.axis_index(axis) for axis in AXES)
    q, b = r // 2, r % 2
    scalars = jnp.stack([2 * m + b, 2 * (1 - q) + c, 2 * q + c, q, b]).astype(jnp.int32)
    pieces = cut(x).reshape(32, rows // 2, cols // CHIPS)
    own = lax.all_to_all(pieces, ("gr", "mat", "gc"), 0, 0, tiled=True)
    own = own.reshape(1024, cols // CHIPS)
    other = send(own, other_core)
    keep, away, panel = gram_strips(scalars, *own_strips(own), own, other)
    gram, late = gather_strips(scalars, sum_strips(keep, away, 1.0 / cols))
    gram, far_first = first_rows(scalars, gram, late, panel)
    far_first = hold(4 * 10**7, send(far_first, home_far))
    (far_second,) = more_rows(1, ((1, 128, 128),), scalars, gram, panel)
    far_second = hold(10**7, send(far_second, home_far))
    near = more_rows(2, ((0, 0, 256), (1, 0, 256)), scalars, gram, panel)
    near = [send(piece, home_near) for piece in near]
    pieces = [v.reshape(-1, 32, cols // CHIPS) for v in (far_first, far_second, *near)]
    return place_rows(scalars, *pieces).reshape(mats, 512, cols // CHIPS)


def solution(mesh):
    fast = tuple(mesh.shape[axis] for axis in AXES) == (4, 4, 2)
    return jax.shard_map(
        fast_body if fast else plain_body,
        mesh=mesh,
        in_specs=(P(None, "gr", ("mat", "gc"), None),),
        out_specs=P(None, "gr", ("mat", "gc")),
        check_vma=False,
    )
```

```python
import functools

import jax
import jax.numpy as jnp
from jax import lax
from jax.experimental import pallas as pl
from jax.experimental.pallas import tpu as pltpu
from jax.sharding import PartitionSpec as P

linear_coef = 3.4445
cubic_coef = -4.775
quintic_coef = 2.0315

AXES = ("mat", "gr", "gc")


def plain_body(iterate):
    regrouped = lax.all_to_all(iterate, ("mat", "gc"), split_axis=3, concat_axis=2, tiled=True)
    row_block = regrouped[:, 0]
    panel_rows = lax.all_gather(row_block, "gr", axis=1, tiled=True)
    total_rows = panel_rows.shape[1]
    groups = lax.axis_size(("mat", "gc"))
    gram_width = total_rows // groups
    inv_cols = 1.0 / iterate.shape[-1]
    partial_value = jnp.einsum(
        "irc,ijc->irj", row_block, panel_rows, preferred_element_type=jnp.float32
    )
    gram_rows = (lax.psum(partial_value, ("mat", "gc")) * inv_cols).astype(jnp.bfloat16)
    own_block = lax.dynamic_slice_in_dim(
        gram_rows, lax.axis_index(("mat", "gc")) * gram_width, gram_width, 2
    )
    square = jnp.einsum(
        "irk,ikj->irj",
        gram_rows,
        lax.all_gather(own_block, "gr", axis=1, tiled=True),
        preferred_element_type=jnp.float32,
    )
    poly_block = (cubic_coef * own_block.astype(jnp.float32) + quintic_coef * square).astype(
        jnp.bfloat16
    )
    mixed_sum = jnp.einsum(
        "irk,ikc->irc",
        lax.all_gather(poly_block, ("mat", "gc"), axis=2, tiled=True),
        panel_rows,
        preferred_element_type=jnp.float32,
    )
    result = linear_coef * row_block.astype(jnp.float32) + mixed_sum
    return result.astype(jnp.bfloat16)


CHIPS = 8
BLOCK = 128
STRIP = 9 * BLOCK
THIRD = STRIP // 3
ORDERS = ((2, 4, 1), (4, 1, 2), (1, 2, 4))
PARAMS = dict(vmem_limit_bytes=28 * 1024 * 1024)


def cost(flops, bytes_accessed):
    return pl.CostEstimate(flops=flops, bytes_accessed=bytes_accessed, transcendentals=0)


def offset(third, place):
    axes = ORDERS[third]
    return sum(axes[k] for k in range(3) if place >> (2 - k) & 1)


def send(value, move):
    perm = []
    for m in range(4):
        for r in range(4):
            for c in range(2):
                to = move(m, r, c)
                perm.append((m * 8 + r * 2 + c, to[0] * 8 + to[1] * 2 + to[2]))
    return lax.ppermute(value, AXES, perm)


def across(d):
    return lambda m, r, c: (m ^ (d >> 1), r ^ (d & 1), c)


def other_core(m, r, c):
    return m, r, 1 - c


def cut_kernel(x_ref, o_ref, sems):
    copies = []
    width = o_ref.shape[-1]
    for q in range(2):
        for k in range(CHIPS):
            copies.append(
                pltpu.make_async_copy(
                    x_ref.at[q, :, pl.ds(k * width, width)],
                    o_ref.at[q, k % 2, k // 2],
                    sems.at[q * CHIPS + k],
                )
            )
    for copy in copies:
        copy.start()
    for copy in copies:
        copy.wait()


def cut(x):
    _, rows, cols = x.shape
    return pl.pallas_call(
        cut_kernel,
        out_shape=jax.ShapeDtypeStruct((2, 2, 4, rows, cols // CHIPS), x.dtype),
        in_specs=[pl.BlockSpec(memory_space=pl.ANY)],
        out_specs=pl.BlockSpec(memory_space=pl.ANY),
        scratch_shapes=[pltpu.SemaphoreType.DMA((16,))],
        compiler_params=pltpu.CompilerParams(**PARAMS),
        name="cut_columns",
    )(x)


GRAM_DIMS = (((1,), (1,)), ((), ()))


def own_kernel(own, strips, panel, sem):
    copy = pltpu.make_async_copy(own, panel.at[pl.ds(0, 1024)], sem)
    copy.start()
    for t in range(4):
        lo = 256 * t
        made = lax.dot_general(
            own[lo : lo + 256, :], own[lo:, :], GRAM_DIMS, preferred_element_type=jnp.float32
        )
        strips[2 * t, :, : 1024 - lo] = made[:BLOCK]
        strips[2 * t + 1, :, : 1024 - BLOCK - lo] = made[BLOCK:, BLOCK:]
    copy.wait()


def own_strips(own):
    rows, cols = own.shape
    return pl.pallas_call(
        own_kernel,
        out_shape=[
            jax.ShapeDtypeStruct((CHIPS, BLOCK, STRIP), jnp.float32),
            jax.ShapeDtypeStruct((2 * rows, cols), own.dtype),
        ],
        in_specs=[pl.BlockSpec(memory_space=pltpu.VMEM)],
        out_specs=[pl.BlockSpec(memory_space=pltpu.VMEM)] * 2,
        scratch_shapes=[pltpu.SemaphoreType.DMA],
        cost_estimate=cost(1024 * 1280 * cols, 10**7),
        compiler_params=pltpu.CompilerParams(**PARAMS),
        name="own_strips",
    )(own)


def gram_kernel(p_ref, strips_in, panel_in, own, other, *rest):
    del strips_in, panel_in
    keep, away, (strips, panel, sem) = rest[:3], rest[3:6], rest[6:]
    copy = pltpu.make_async_copy(other, panel.at[pl.ds(1024, 1024)], sem)
    copy.start()
    for t in range(4):
        lo = 256 * t
        made = lax.dot_general(
            own[lo : lo + 256, :],
            other[: lo + 256, :],
            GRAM_DIMS,
            preferred_element_type=jnp.float32,
        )
        strips[2 * t, :, 1024 - lo :] = made[:BLOCK, : BLOCK + lo]
        strips[2 * t + 1, :, 1024 - BLOCK - lo :] = made[BLOCK:]
    p = p_ref[0]
    for i in range(3):
        cols = slice(THIRD * i, THIRD * (i + 1))
        for place in range(4):
            keep[i][place] = strips[p ^ offset(i, place), :, cols]
            away[i][place] = strips[p ^ offset(i, place + 4), :, cols].astype(jnp.bfloat16)
    copy.wait()


def gram_strips(p, strips, panel, own, other):
    shape = (4, BLOCK, THIRD)
    made = pl.pallas_call(
        gram_kernel,
        out_shape=[jax.ShapeDtypeStruct(shape, jnp.float32)] * 3
        + [jax.ShapeDtypeStruct(shape, jnp.bfloat16)] * 3
        + [jax.ShapeDtypeStruct(v.shape, v.dtype) for v in (strips, panel)],
        in_specs=[pl.BlockSpec(memory_space=pltpu.SMEM)]
        + [pl.BlockSpec(memory_space=pltpu.VMEM)] * 4,
        out_specs=[pl.BlockSpec(memory_space=pltpu.VMEM)] * 8,
        scratch_shapes=[pltpu.SemaphoreType.DMA],
        input_output_aliases={1: 6, 2: 7},
        cost_estimate=cost(1024 * 1280 * own.shape[-1], 10**7),
        compiler_params=pltpu.CompilerParams(**PARAMS),
        name="gram_strips",
    )(p, strips, panel, own, other)
    return made[:3], made[3:6], made[7]


def halves_kernel(held, came, keep, away):
    half = keep.shape[0]
    total = held[...] + came[...].astype(jnp.float32)
    keep[...] = total[:half]
    away[...] = total[half:].astype(jnp.bfloat16)


def pairs_kernel(held, came, keep, away):
    total = held[...] + came[...].astype(jnp.float32)
    keep[...] = total
    away[0] = total[1].astype(jnp.bfloat16)
    away[1] = total[0].astype(jnp.bfloat16)


def last_kernel(scale, held, came, out):
    total = held[...] + came[...].astype(jnp.float32)
    out[...] = (total * scale).astype(jnp.bfloat16)


def add(kernel, name, types, held, came):
    shape = (2, BLOCK, THIRD)
    return pl.pallas_call(
        kernel,
        out_shape=[jax.ShapeDtypeStruct(shape, dtype) for dtype in types],
        in_specs=[pl.BlockSpec(memory_space=pltpu.VMEM)] * 2,
        out_specs=[pl.BlockSpec(memory_space=pltpu.VMEM)] * len(types),
        cost_estimate=cost(10**5, 10**6),
        compiler_params=pltpu.CompilerParams(**PARAMS),
        name=name,
    )(held, came)


def sum_third(third, keep, away, scale):
    first, second, last = (across(axis) for axis in ORDERS[third])
    both = (jnp.float32, jnp.bfloat16)
    keep, away = add(halves_kernel, "add_halves", both, keep, send(away, first))
    keep, away = add(pairs_kernel, "add_pairs", both, keep, send(away, second))
    (made,) = add(
        functools.partial(last_kernel, scale), "add_last", both[1:], keep, send(away, last)
    )
    return made


def sum_strips(keep, away, scale):
    return [sum_third(third, keep[third], away[third], scale) for third in range(3)]


def gather_strips(scalars, parts):
    came = [send(parts[i], across(ORDERS[i][1])) for i in range(3)]
    early = [jnp.concatenate([parts[i], came[i]], axis=0) for i in range(3)]
    late = [send(early[i], across(ORDERS[i][0])) for i in range(3)]
    early += [send(part, other_core) for part in early]
    gram = early_gram(scalars, early, late[0])
    return gram, late + [send(part, other_core) for part in late]


def fill(gram, p, thirds, first_place):
    for k, ref in enumerate(thirds):
        third, far_half = k % 3, 8 * (k // 3)
        for j in range(4):
            row = (p ^ offset(third, first_place + j)) + far_half
            row_at = pl.ds(pl.multiple_of(row * BLOCK, BLOCK), BLOCK)
            for d in range(3 * third, 3 * third + 3):
                col = (row + d) & 15
                col_at = pl.ds(pl.multiple_of(col * BLOCK, BLOCK), BLOCK)
                block = ref[j, :, BLOCK * (d - 3 * third) : BLOCK * (d - 3 * third + 1)]
                gram[row_at, col_at] = block
                if 1 <= d <= 7:
                    gram[col_at, row_at] = block.T


def early_kernel(s_ref, *refs):
    fill(refs[7], s_ref[0], refs[:6], 0)


def early_gram(scalars, early, first_late):
    return pl.pallas_call(
        early_kernel,
        out_shape=jax.ShapeDtypeStruct((2048, 2048), jnp.bfloat16),
        in_specs=[pl.BlockSpec(memory_space=pltpu.SMEM)]
        + [pl.BlockSpec(memory_space=pltpu.VMEM)] * 6
        + [pl.BlockSpec(memory_space=pl.ANY)],
        out_specs=pl.BlockSpec(memory_space=pltpu.VMEM),
        cost_estimate=cost(10**5, 3 * 10**7),
        compiler_params=pltpu.CompilerParams(**PARAMS),
        name="early_gram",
    )(scalars, *early, first_late)


def result_rows(gram, panel, poly, place, half, first, count):
    start = pl.multiple_of(1024 * half + place * 256 + first, BLOCK)
    rows = gram[pl.ds(start, count), :]
    for n in range(0, 2048, 512):
        square = jnp.dot(rows, gram[:, n : n + 512], preferred_element_type=jnp.float32)
        poly[:count, n : n + 512] = (
            cubic_coef * rows[:, n : n + 512].astype(jnp.float32) + quintic_coef * square
        ).astype(jnp.bfloat16)
    mixed = jnp.dot(poly[:count], panel[...], preferred_element_type=jnp.float32)
    return (linear_coef * panel[pl.ds(start, count), :].astype(jnp.float32) + mixed).astype(
        jnp.bfloat16
    )


def first_kernel(s_ref, *refs):
    late, gram_in, panel, gram, out, poly = refs[:6], *refs[6:]
    del gram_in
    fill(gram, s_ref[0], late, 4)
    out[:256] = result_rows(gram, panel, poly, s_ref[1], 0, 0, 256)
    out[256:] = result_rows(gram, panel, poly, s_ref[1], 1, 0, 128)


def first_rows(scalars, gram, late, panel):
    cols = panel.shape[-1]
    return pl.pallas_call(
        first_kernel,
        out_shape=[
            jax.ShapeDtypeStruct((2048, 2048), jnp.bfloat16),
            jax.ShapeDtypeStruct((384, cols), jnp.bfloat16),
        ],
        in_specs=[pl.BlockSpec(memory_space=pltpu.SMEM)]
        + [pl.BlockSpec(memory_space=pltpu.VMEM)] * 8,
        out_specs=[pl.BlockSpec(memory_space=pltpu.VMEM)] * 2,
        scratch_shapes=[pltpu.VMEM((256, 2048), jnp.bfloat16)],
        input_output_aliases={7: 0},
        cost_estimate=cost(2 * 384 * 2048 * (2048 + cols), 3 * 10**7),
        compiler_params=pltpu.CompilerParams(**PARAMS),
        name="first_rows",
    )(scalars, *late, gram, panel)


def more_kernel(scalar, parts, s_ref, gram, panel, *rest):
    outs, poly = rest[:-1], rest[-1]
    for part, out in zip(parts, outs, strict=True):
        out[...] = result_rows(gram, panel, poly, s_ref[scalar], *part)


def more_rows(scalar, parts, scalars, gram, panel):
    cols = panel.shape[-1]
    rows = sum(part[2] for part in parts)
    return pl.pallas_call(
        functools.partial(more_kernel, scalar, parts),
        out_shape=[jax.ShapeDtypeStruct((part[2], cols), jnp.bfloat16) for part in parts],
        in_specs=[pl.BlockSpec(memory_space=pltpu.SMEM)]
        + [pl.BlockSpec(memory_space=pltpu.VMEM)] * 2,
        out_specs=[pl.BlockSpec(memory_space=pltpu.VMEM)] * len(parts),
        scratch_shapes=[pltpu.VMEM((256, 2048), jnp.bfloat16)],
        cost_estimate=cost(2 * rows * 2048 * (2048 + cols), 10**7),
        compiler_params=pltpu.CompilerParams(**PARAMS),
        name="more_rows",
    )(scalars, gram, panel)


def hold_kernel(*refs):
    del refs


def hold(bytes_moved, piece, *earlier):
    return pl.pallas_call(
        hold_kernel,
        out_shape=jax.ShapeDtypeStruct(piece.shape, piece.dtype),
        in_specs=[pl.BlockSpec(memory_space=pl.ANY)] * (1 + len(earlier)),
        out_specs=pl.BlockSpec(memory_space=pl.ANY),
        input_output_aliases={0: 0},
        cost_estimate=cost(10**6, bytes_moved),
        compiler_params=pltpu.CompilerParams(**PARAMS),
        name="hold",
    )(piece, *earlier)


def place_kernel(s_ref, far_first, far_second, near_own, near_other, out, sems):
    matrix, core = s_ref[3], s_ref[4]
    moves = (
        (far_first.at[0:8], out.at[1 - matrix, :, core]),
        (far_first.at[8:12], out.at[1 - matrix, 0:4, 1 - core]),
        (far_second, out.at[1 - matrix, 4:8, 1 - core]),
        (near_own, out.at[matrix, :, core]),
        (near_other, out.at[matrix, :, 1 - core]),
    )
    copies = []
    for source, target in moves:
        for k in range(0, source.shape[0], 2):
            pair = pl.ds(k, 2)
            sem = sems.at[len(copies)]
            copies.append(pltpu.make_async_copy(source.at[pair], target.at[pair], sem))
    for copy in copies:
        copy.start()
    for copy in copies:
        copy.wait()


def place_rows(scalars, *pieces):
    _, rows, cols = pieces[0].shape
    return pl.pallas_call(
        place_kernel,
        out_shape=jax.ShapeDtypeStruct((2, 8, 2, rows, cols), jnp.bfloat16),
        in_specs=[pl.BlockSpec(memory_space=pltpu.SMEM)]
        + [pl.BlockSpec(memory_space=pl.ANY)] * len(pieces),
        out_specs=pl.BlockSpec(memory_space=pl.ANY),
        scratch_shapes=[pltpu.SemaphoreType.DMA((16,))],
        compiler_params=pltpu.CompilerParams(**PARAMS),
        name="place_rows",
    )(scalars, *pieces)


def home_far(m, r, c):
    return m, (1 - r // 2) * 2 + c, r % 2


def home_near(m, r, c):
    return m, (r // 2) * 2 + c, r % 2


def fast_body(iterate):
    x = iterate[:, 0]
    mats, rows, cols = x.shape
    m, r, c = (lax.axis_index(axis) for axis in AXES)
    q, b = r // 2, r % 2
    scalars = jnp.stack([2 * m + b, 2 * (1 - q) + c, 2 * q + c, q, b]).astype(jnp.int32)
    pieces = cut(x).reshape(32, rows // 2, cols // CHIPS)
    own = lax.all_to_all(pieces, ("gr", "mat", "gc"), 0, 0, tiled=True)
    own = own.reshape(1024, cols // CHIPS)
    other = send(own, other_core)
    keep, away, panel = gram_strips(scalars, *own_strips(own), own, other)
    gram, late = gather_strips(scalars, sum_strips(keep, away, 1.0 / cols))
    gram, far_first = first_rows(scalars, gram, late, panel)
    far_first = hold(4 * 10**7, send(far_first, home_far))
    (far_second,) = more_rows(1, ((1, 128, 128),), scalars, gram, panel)
    far_second = hold(10**7, send(far_second, home_far))
    near = more_rows(2, ((0, 0, 256), (1, 0, 256)), scalars, gram, panel)
    near = [send(piece, home_near) for piece in near]
    pieces = [v.reshape(-1, 32, cols // CHIPS) for v in (far_first, far_second, *near)]
    return place_rows(scalars, *pieces).reshape(mats, 512, cols // CHIPS)


def solution(mesh):
    fast = tuple(mesh.shape[axis] for axis in AXES) == (4, 4, 2)
    return jax.shard_map(
        fast_body if fast else plain_body,
        mesh=mesh,
        in_specs=(P(None, "gr", ("mat", "gc"), None),),
        out_specs=P(None, "gr", ("mat", "gc")),
        check_vma=False,
    )
```
